32 devices in a mesh: groups: 2 (over x), gx: 16 (over z, y, core).
Axes of the slice: x: 2, y: 2, z: 4, core: 2. Of those that a mesh axis runs over, the one named last changes fastest.
Arguments:
- hidden: bfloat16 [256, 18432], P('groups', 'gx'), parts along dimension 0, may hold values from -28 to 28, as said below
- w_qkv: bfloat16 [147456, 2688], P('gx'), may hold values from -0.046875 to 0.046875
- w_out: bfloat16 [147456, 2304], P('gx'), may hold values from -0.046875 to 0.046875
- segment_ids: int32 [256], P('groups'), parts along dimension 0, may hold values from 0 to 3, as said below
- end_positions: int32 [8], P('groups'), parts along dimension 0, may hold values from 0 to 127, as said below
- owners: int32 [8], P('groups'), parts along dimension 0, may hold values from 0 to 15, as said below
Outputs:
- mixed: bfloat16 [256, 18432], P('groups', 'gx'), parts along dimension 0
- reward_rows: bfloat16 [64, 18432], P(('groups', 'gx')), parts along dimension 0
The draws below stay inside these ranges and needn't reach their ends.
There are 2 independent parts, one for each index of `groups`. The reference program is written for one: setup_inputs(seed, part) draws one part's arguments, and reference() takes and returns one part's arrays. A program takes and returns all parts, laid end to end along the dimension named above; an argument that names none is the same for every part. Nothing has to cross between parts.
Inputs may be any that keep to these rules, and one draw needn't show every extreme that they name: `hidden`: activations of the span's tokens. `segment_ids`: completion numbers never fall along the span, start at 0 and end at 3, each used by one or more tokens. end_positions[c] is the last token with segment_ids equal to c. `owners`: no device owns more than 2 completions; some device owns exactly 2.
All inputs are finite; a program needn't handle non-finite values.
Results may differ from the reference program's by a relative error of at most 0.012.
Values may be sent and summed in bfloat16 or wider, within the bound.
No kernel may reach another device: no remote copies, remote signals or barrier semaphores. Data moves between devices by JAX's collectives and lax.ppermute only.
A program may use at most 192 MiB of HBM per device.

```python
import math
import jax
import jax.numpy as jnp
from jax import lax

D = 18432
HD = 192
HPG = 12
KVG = 8
SLOTS = 2
TOKENS = 128
DOCS = 4
N_GX = 16


def document_cuts(key):
    cut_key = jax.random.fold_in(key, 5)
    shuffled = jax.random.permutation(cut_key, TOKENS - 1)[:DOCS - 1] + 1
    return jnp.sort(shuffled).astype(jnp.int32)


def draw_hidden(key, part):
    key = jax.random.fold_in(key, 11)
    first_key = jax.random.fold_in(key, 0)
    sample = jnp.clip(jax.random.normal(first_key, (TOKENS, D), jnp.float32), -6.0, 6.0)
    return sample.astype(jnp.bfloat16)


def draw_segment_ids(key, part):
    cut_list = document_cuts(key)
    positions = jnp.arange(TOKENS, dtype=jnp.int32)
    return jnp.sum((positions[:, None] >= cut_list[None, :]).astype(jnp.int32), axis=1).astype(jnp.int32)


def draw_end_positions(key, part):
    cut_list = document_cuts(key)
    return jnp.concatenate([cut_list - 1, jnp.array([TOKENS - 1], jnp.int32)]).astype(jnp.int32)


def draw_owners(key, part):
    key = jax.random.fold_in(key, 7)
    first_key, second_key, third_key = jax.random.split(key, 3)
    shuffled = jax.random.permutation(first_key, N_GX)[:DOCS].astype(jnp.int32)
    source = jax.random.randint(second_key, (), 0, DOCS)
    target = (source + jax.random.randint(third_key, (), 1, DOCS)) % DOCS
    return shuffled.at[target].set(shuffled[source]).astype(jnp.int32)


def block_scale(own_key, extent, cuts, low, largest):
    loudness, own = 1.0, jax.random.fold_in(own_key, 6)
    for position, blocks in cuts:
        draws = jnp.exp(jax.random.uniform(jax.random.fold_in(own, position), (blocks,), jnp.float32, low / len(cuts), largest / len(cuts)))
        loudness = loudness * jnp.repeat(draws, extent[position] // blocks).reshape([-1 if axis == position else 1 for axis in range(len(extent))])
    return loudness


def bell_draw(key, extent, spread, bound, cuts=(), kind=jnp.bfloat16):
    values = spread * jax.random.normal(key, extent, jnp.float32)
    if cuts:
        values = values * block_scale(key, extent, cuts, -0.22, 0.18)
    return jnp.clip(values, -bound, bound).astype(kind)


def setup_inputs(seed: int = 0, part: int = 0) -> dict:
    splits = jax.random.split(jax.random.key(seed), 7)
    part_splits = jax.random.split(jax.random.fold_in(splits[6], part), 7)
    return {
        "hidden": draw_hidden(jax.random.fold_in(jax.random.fold_in(splits[6], part), 71), part),
        "w_qkv": bell_draw(splits[1], (D * KVG, (HPG + 2) * HD), D ** -0.5, 0.046875, ((0, 16),)),
        "w_out": bell_draw(splits[2], (D * KVG, HPG * HD), (HPG * HD * KVG) ** -0.5, 0.046875, ((0, 16),)),
        "segment_ids": draw_segment_ids(jax.random.fold_in(jax.random.fold_in(splits[6], part), 71), part),
        "end_positions": draw_end_positions(jax.random.fold_in(jax.random.fold_in(splits[6], part), 71), part),
        "owners": draw_owners(jax.random.fold_in(jax.random.fold_in(splits[6], part), 71), part),
    }


def contract_last(left, right):
    return lax.dot_general(left, right, (((1,), (1,)), ((), ())), preferred_element_type=jnp.float32)

def reference(hidden, w_qkv, w_out, segment_ids, end_positions, owners):
    tokens = hidden.shape[0]
    row_blocks = N_GX // KVG
    block_width = D // row_blocks
    query_width = HPG * HD
    in_blocks = w_qkv.reshape(row_blocks, KVG, block_width, (HPG + 2) * HD)
    out_blocks = w_out.reshape(row_blocks, KVG, block_width, query_width)
    positions = jnp.arange(tokens)
    allowed = (segment_ids[:, None] == segment_ids[None, :]) & (positions[None, :] <= positions[:, None])
    row_allowed = jnp.repeat(allowed, HPG, axis=0)
    scale = 1.0 / math.sqrt(HD)

    def one_group(running, group_index):
        group_weights = lax.dynamic_index_in_dim(in_blocks, group_index, 1, keepdims=False).reshape(D, (HPG + 2) * HD)
        projected = jnp.dot(hidden, group_weights, preferred_element_type=jnp.float32).astype(jnp.bfloat16)
        queries = projected[:, :query_width].reshape(tokens * HPG, HD)
        key_block = projected[:, query_width:query_width + HD]
        value_block = projected[:, query_width + HD:]
        scores = contract_last(queries, key_block) * scale
        row_max = lax.optimization_barrier(jnp.max(jnp.where(row_allowed, scores, -jnp.inf), axis=1, keepdims=True))
        weights = jnp.where(row_allowed, jnp.exp(scores - row_max), 0.0)
        totals = lax.optimization_barrier(jnp.sum(weights, axis=1, keepdims=True))
        mixed_heads = jnp.dot(weights.astype(jnp.bfloat16), value_block, preferred_element_type=jnp.float32)
        attended = (mixed_heads / totals).astype(jnp.bfloat16).reshape(tokens, query_width)
        out_weights = lax.dynamic_index_in_dim(out_blocks, group_index, 1, keepdims=False).reshape(D, query_width)
        return (running + contract_last(attended, out_weights), None)
    running, unused = lax.scan(one_group, jnp.zeros((tokens, D), jnp.float32), jnp.arange(KVG))
    mixed = running.astype(jnp.bfloat16)
    completions = owners.shape[0]
    picked = jnp.take(mixed, end_positions, axis=0)
    same_owner = owners[:, None] == owners[None, :]
    earlier = jnp.arange(completions)[None, :] < jnp.arange(completions)[:, None]
    order_rank = lax.optimization_barrier(jnp.sum((same_owner & earlier).astype(jnp.int32), axis=1)).astype(jnp.int32)
    target = owners * SLOTS + order_rank
    chooser = (target[None, :] == jnp.arange(N_GX * SLOTS)[:, None]).astype(jnp.bfloat16)
    reward_rows = jnp.dot(chooser, picked, preferred_element_type=jnp.float32).astype(jnp.bfloat16)
    return (mixed, reward_rows)
```

```python
import math

import jax
import jax.numpy as jnp
from jax import lax
from jax.experimental import pallas as pl
from jax.experimental.pallas import tpu as pltpu
from jax.sharding import PartitionSpec as P

HD = 192
HPG = 12
KVG = 8
SLOTS = 2


def from_partner(block, axis, distance):
    count = lax.axis_size(axis)
    route = []
    for low in range(count):
        high = low | 1 << distance
        if high != low and high < count:
            route += [(low, high), (high, low)]
    return lax.ppermute(block, axis, route)


def join_pair(mine, partner, upper_bit, axis_number):
    return jnp.where(
        upper_bit == 1,
        jnp.concatenate([partner, mine], axis_number),
        jnp.concatenate([mine, partner], axis_number),
    )


def halve_pick(current, upper_bit, axis_number):
    half_rows = current.shape[axis_number] // 2
    low_half = lax.slice_in_dim(current, 0, half_rows, axis=axis_number)
    high_half = lax.slice_in_dim(current, half_rows, 2 * half_rows, axis=axis_number)
    outgoing = jnp.where(upper_bit == 1, low_half, high_half)
    kept_half = jnp.where(upper_bit == 1, high_half, low_half)
    return (outgoing, kept_half)


def contract_last(left, right):
    return lax.dot_general(
        left, right, (((1,), (1,)), ((), ())), preferred_element_type=jnp.float32
    )


def general_device(hidden, w_qkv, w_out, segment_ids, end_positions, owners):
    devices = lax.axis_size("gx")
    blocks = devices // KVG
    group_bits = KVG.bit_length() - 1
    block_bits = blocks.bit_length() - 1
    my_index = lax.axis_index("gx")
    my_group = my_index % KVG
    my_block = my_index // KVG
    tokens = hidden.shape[0]
    query_width = HPG * HD
    block_rows = tokens // blocks
    scale = 1.0 / math.sqrt(HD)
    features = hidden
    for bit_number in range(group_bits):
        partner = from_partner(features, "gx", bit_number)
        features = join_pair(features, partner, my_group >> bit_number & 1, 1)
    partial_value = jnp.dot(features, w_qkv, preferred_element_type=jnp.float32)
    local_part = partial_value
    for level in reversed(range(block_bits)):
        outgoing, kept_half = halve_pick(local_part, my_block >> level & 1, 0)
        local_part = kept_half + from_partner(outgoing, "gx", group_bits + level)
    query_part = local_part[:, :query_width]
    pair_rows = local_part[:, query_width:].astype(jnp.bfloat16)
    for level in range(block_bits):
        partner = from_partner(pair_rows, "gx", group_bits + level)
        pair_rows = join_pair(pair_rows, partner, my_block >> level & 1, 0)
    key_block = pair_rows[:, :HD]
    value_block = pair_rows[:, HD:]
    queries = query_part.astype(jnp.bfloat16).reshape(block_rows * HPG, HD)
    start = my_block * block_rows
    my_segments = lax.dynamic_slice_in_dim(segment_ids, start, block_rows)
    row_segments = jnp.repeat(my_segments, HPG)
    row_positions = start + jnp.repeat(jnp.arange(block_rows, dtype=jnp.int32), HPG)
    positions = jnp.arange(tokens, dtype=jnp.int32)
    allowed = (row_segments[:, None] == segment_ids[None, :]) & (
        positions[None, :] <= row_positions[:, None]
    )
    scores, allowed = (contract_last(queries, key_block) * scale, allowed)
    row_max = jnp.max(jnp.where(allowed, scores, -jnp.inf), axis=1, keepdims=True)
    weights = jnp.where(allowed, jnp.exp(scores - row_max), 0.0)
    totals = jnp.sum(weights, axis=1, keepdims=True)
    mixed_heads = jnp.dot(
        weights.astype(jnp.bfloat16), value_block, preferred_element_type=jnp.float32
    )
    attended = (mixed_heads / totals).astype(jnp.bfloat16).reshape(block_rows, query_width)
    for level in range(block_bits):
        partner = from_partner(attended, "gx", group_bits + level)
        attended = join_pair(attended, partner, my_block >> level & 1, 0)
    output_part = contract_last(attended, w_out)
    for bit_number in reversed(range(group_bits)):
        outgoing, kept_half = halve_pick(output_part, my_group >> bit_number & 1, 1)
        output_part = kept_half + from_partner(outgoing, "gx", bit_number)
    mixed = output_part.astype(jnp.bfloat16)
    picker = (end_positions[:, None] == jnp.arange(tokens, dtype=jnp.int32)[None, :]).astype(
        jnp.bfloat16
    )
    end_local = jnp.dot(picker, mixed, preferred_element_type=jnp.float32).astype(jnp.bfloat16)
    end_full = lax.all_gather(end_local, "gx", axis=1, tiled=True)
    completions = owners.shape[0]
    same_owner = owners[:, None] == owners[None, :]
    earlier = jnp.arange(completions)[None, :] < jnp.arange(completions)[:, None]
    order_rank = jnp.sum((same_owner & earlier).astype(jnp.int32), axis=1)
    chooser = (
        (owners[None, :] == my_index)
        & (order_rank[None, :] == jnp.arange(SLOTS, dtype=jnp.int32)[:, None])
    ).astype(jnp.bfloat16)
    reward_rows = jnp.dot(chooser, end_full, preferred_element_type=jnp.float32).astype(
        jnp.bfloat16
    )
    return (mixed, reward_rows)


CHUNKS = (4, 4, 4)
VMEM_BYTES = 50 * 1024 * 1024


def xor_swap(block, distance):
    count = lax.axis_size("gx")
    return lax.ppermute(block, "gx", [(low, low ^ distance) for low in range(count)])


def in_vmem():
    return pl.BlockSpec(memory_space=pltpu.VMEM)


def project(features, distances, running, w_qkv, my_group):
    tokens, width = features[0].shape
    columns = w_qkv.shape[1]
    count = len(features)
    block_ids = jnp.stack([my_group ^ d for d in distances]).astype(jnp.int32)

    def kernel(ids_ref, *refs):
        feature_refs = refs[:count]
        w_ref = refs[count]
        start_ref = refs[count + 1] if running is not None else None
        out_ref, current = refs[-2:]
        step = pl.program_id(0)
        for i in range(count):

            @pl.when(step == i)
            def _():
                current[...] = feature_refs[i][...]

        @pl.when(step == 0)
        def _():
            out_ref[...] = jnp.zeros_like(out_ref) if start_ref is None else start_ref[...]

        out_ref[...] += jnp.dot(current[...], w_ref[...], preferred_element_type=jnp.float32)

    whole = pl.BlockSpec((tokens, width), lambda i, ids: (0, 0))
    total = pl.BlockSpec((tokens, columns), lambda i, ids: (0, 0))
    operands = list(features) + [w_qkv] + ([] if running is None else [running])
    return pl.pallas_call(
        kernel,
        grid_spec=pltpu.PrefetchScalarGridSpec(
            num_scalar_prefetch=1,
            grid=(count,),
            in_specs=[whole] * count
            + [pl.BlockSpec((width, columns), lambda i, ids: (ids[i], 0))]
            + ([] if running is None else [total]),
            out_specs=total,
            scratch_shapes=[pltpu.VMEM((tokens, width), jnp.bfloat16)],
        ),
        out_shape=jax.ShapeDtypeStruct((tokens, columns), jnp.float32),
        compiler_params=pltpu.CompilerParams(vmem_limit_bytes=VMEM_BYTES),
        cost_estimate=pl.CostEstimate(
            flops=2 * count * tokens * width * columns,
            bytes_accessed=2 * count * width * columns,
            transcendentals=0,
        ),
        name="project",
    )(block_ids, *operands)


def attend_and_mix(own_queries, partner_queries, keys, values, allowed, running, w_out, first, my_group, last, picker):
    tokens, chunk_width = own_queries.shape
    heads = chunk_width // HD
    rows = w_out.shape[0] // KVG
    block_ids = (my_group ^ jnp.arange(KVG, dtype=jnp.int32)).astype(jnp.int32)
    scale = 1.0 / math.sqrt(HD)
    column_block = first * HD // chunk_width

    def kernel(ids_ref, own_ref, partner_ref, key_ref, value_ref, allowed_ref, w_ref, *refs):
        refs = list(refs)
        start_ref = refs.pop(0) if running is not None else None
        picker_ref = refs.pop(0) if last else None
        out_ref = refs.pop(0)
        end_ref = refs.pop(0) if last else None
        attended = refs.pop(0)
        step = pl.program_id(0)

        @pl.when(step == 0)
        def _():
            queries = (own_ref[...] + partner_ref[...].astype(jnp.float32)).astype(jnp.bfloat16)
            mask = allowed_ref[...] > 0.0
            for head in range(heads):
                lanes = slice(head * HD, (head + 1) * HD)
                scores = contract_last(queries[:, lanes], key_ref[...]) * scale
                row_max = jnp.max(jnp.where(mask, scores, -jnp.inf), axis=1, keepdims=True)
                weights = jnp.where(mask, jnp.exp(scores - row_max), 0.0)
                totals = jnp.sum(weights, axis=1, keepdims=True)
                mixed_heads = jnp.dot(
                    weights.astype(jnp.bfloat16), value_ref[...], preferred_element_type=jnp.float32
                )
                attended[:, lanes] = (mixed_heads / totals).astype(jnp.bfloat16)

        part = contract_last(attended[...], w_ref[...])
        if start_ref is not None:
            part += start_ref[step]
        out_ref[step] = part.astype(out_ref.dtype)
        if last:
            end_ref[step] = jnp.dot(
                picker_ref[...], part.astype(jnp.bfloat16), preferred_element_type=jnp.float32
            )

    def whole(shape):
        return pl.BlockSpec(shape, lambda i, ids: (0,) * len(shape))

    out_dims = (KVG, tokens, rows)
    out_shape = [jax.ShapeDtypeStruct(out_dims, jnp.bfloat16 if last else jnp.float32)]
    out_specs = [whole(out_dims)]
    operands = [own_queries, partner_queries, keys, values, allowed, w_out]
    in_specs = [whole(o.shape) for o in operands[:-1]]
    in_specs.append(pl.BlockSpec((rows, chunk_width), lambda i, ids: (ids[i], column_block)))
    if running is not None:
        operands.append(running)
        in_specs.append(whole(out_dims))
    if last:
        operands.append(picker)
        in_specs.append(whole(picker.shape))
        end_dims = (KVG, picker.shape[0], rows)
        out_shape.append(jax.ShapeDtypeStruct(end_dims, jnp.float32))
        out_specs.append(whole(end_dims))
    result = pl.pallas_call(
        kernel,
        grid_spec=pltpu.PrefetchScalarGridSpec(
            num_scalar_prefetch=1,
            grid=(KVG,),
            in_specs=in_specs,
            out_specs=out_specs,
            scratch_shapes=[pltpu.VMEM((tokens, chunk_width), jnp.bfloat16)],
        ),
        out_shape=out_shape,
        compiler_params=pltpu.CompilerParams(vmem_limit_bytes=VMEM_BYTES),
        cost_estimate=pl.CostEstimate(
            flops=2 * KVG * tokens * rows * chunk_width,
            bytes_accessed=2 * KVG * rows * chunk_width,
            transcendentals=heads * tokens * tokens,
        ),
        name="attend_and_mix",
    )(block_ids, *operands)
    return result if last else result[0]


def swap_blocks(blocks, distance):
    return [blocks[j ^ distance] for j in range(len(blocks))]


def natural_order(blocks, my_group):
    distance = 1
    while distance < len(blocks):
        bit = my_group // distance % 2 == 1
        swapped = swap_blocks(blocks, distance)
        blocks = [jnp.where(bit, other, own) for own, other in zip(blocks, swapped)]
        distance *= 2
    return jnp.concatenate(blocks, axis=-1)


def pair_device(hidden, w_qkv, w_out, segment_ids, end_positions, owners):
    my_index = lax.axis_index("gx")
    my_group = my_index % KVG
    my_block = my_index // KVG
    tokens = hidden.shape[0]
    query_width = HPG * HD
    positions = jnp.arange(tokens, dtype=jnp.int32)
    allowed = (
        (segment_ids[:, None] == segment_ids[None, :]) & (positions[None, :] <= positions[:, None])
    ).astype(jnp.float32)
    completions = owners.shape[0]
    end_rows = -(-completions // 8) * 8
    picker = (
        jnp.pad(end_positions, (0, end_rows - completions), constant_values=-1)[:, None] == positions[None, :]
    ).astype(jnp.bfloat16)

    features = {0: hidden}
    for distance in range(2, KVG, 2):
        features[distance] = xor_swap(hidden, distance)
    for distance in range(0, KVG, 2):
        features[distance + 1] = xor_swap(features[distance], 1)
    early, late = (0, 1), tuple(range(2, KVG))
    partial = project([features[d] for d in early], early, None, w_qkv, my_group)
    partial = project([features[d] for d in late], late, partial, w_qkv, my_group)

    rounded = partial.astype(jnp.bfloat16)
    lanes = []
    low = 0
    for heads in CHUNKS:
        lanes.append((low, low + heads * HD))
        low += heads * HD
    partner_kv = xor_swap(rounded[:, query_width:], KVG)
    partner_queries = [xor_swap(rounded[:, low:high], KVG) for low, high in lanes]
    pair = (partial[:, query_width:] + partner_kv.astype(jnp.float32)).astype(jnp.bfloat16)
    keys, values = pair[:, :HD], pair[:, HD:]
    running = None
    for number, (low, high) in enumerate(lanes):
        last = number == len(lanes) - 1
        running = attend_and_mix(
            partial[:, low:high],
            partner_queries[number],
            keys,
            values,
            allowed,
            running,
            w_out,
            low // HD,
            my_group,
            last,
            picker,
        )
    parts, end_parts = running

    end_parts = end_parts[:, :completions].astype(jnp.bfloat16)
    near = [end_parts[j].astype(jnp.float32) for j in range(0, KVG, 2)]
    far = xor_swap(end_parts[1::2], 1).astype(jnp.float32)
    near = [(mine + far[i]) for i, mine in enumerate(near)]
    message = jnp.stack(near).astype(jnp.bfloat16)
    ends = list(near)
    for distance in range(2, KVG, 2):
        arrived = xor_swap(message, distance).astype(jnp.float32)
        arrived = swap_blocks([arrived[i] for i in range(KVG // 2)], distance // 2)
        ends = [a + b for a, b in zip(ends, arrived)]
    ends = jnp.stack(ends).astype(jnp.bfloat16)
    both = jnp.stack([ends, xor_swap(ends, KVG)])
    both_far = xor_swap(both, 1)
    halves = []
    for half in range(2):
        blocks = []
        for i in range(KVG // 2):
            blocks += [both[half, i], both_far[half, i]]
        halves.append(natural_order(blocks, my_group))
    end_full = jnp.concatenate(
        [jnp.where(my_block == 0, halves[0], halves[1]), jnp.where(my_block == 0, halves[1], halves[0])], axis=-1
    )
    same_owner = owners[:, None] == owners[None, :]
    earlier = jnp.arange(completions)[None, :] < jnp.arange(completions)[:, None]
    order_rank = jnp.sum((same_owner & earlier).astype(jnp.int32), axis=1)
    chooser = (
        (owners[None, :] == my_index)
        & (order_rank[None, :] == jnp.arange(SLOTS, dtype=jnp.int32)[:, None])
    ).astype(jnp.bfloat16)
    reward_rows = jnp.dot(chooser, end_full, preferred_element_type=jnp.float32).astype(jnp.bfloat16)

    arrived = xor_swap(parts[1::2], 1)
    near = parts[0::2].astype(jnp.float32) + arrived.astype(jnp.float32)
    mixed = near[0]
    for distance in range(2, KVG, 2):
        mixed += xor_swap(near[distance // 2].astype(jnp.bfloat16), distance).astype(jnp.float32)
    return (mixed.astype(jnp.bfloat16), reward_rows)


def per_device(hidden, w_qkv, w_out, segment_ids, end_positions, owners):
    tokens, width = hidden.shape
    blocks = lax.axis_size("gx") // KVG
    if blocks == 2 and width % 128 == 0 and tokens % 16 == 0 and tokens <= 128:
        return pair_device(hidden, w_qkv, w_out, segment_ids, end_positions, owners)
    return general_device(hidden, w_qkv, w_out, segment_ids, end_positions, owners)


def solution(mesh):
    placed = (
        P("groups", "gx"),
        P("gx", None),
        P("gx", None),
        P("groups"),
        P("groups"),
        P("groups"),
    )
    return jax.shard_map(
        per_device,
        mesh=mesh,
        in_specs=placed,
        out_specs=(P("groups", "gx"), P(("groups", "gx"), None)),
        check_vma=False,
    )
```

```python
import math

import jax
import jax.numpy as jnp
from jax import lax
from jax.experimental import pallas as pl
from jax.experimental.pallas import tpu as pltpu
from jax.sharding import PartitionSpec as P

HD = 192
HPG = 12
KVG = 8
SLOTS = 2


def from_partner(block, axis, distance):
    count = lax.axis_size(axis)
    route = []
    for low in range(count):
        high = low | 1 << distance
        if high != low and high < count:
            route += [(low, high), (high, low)]
    return lax.ppermute(block, axis, route)


def join_pair(mine, partner, upper_bit, axis_number):
    return jnp.where(
        upper_bit == 1,
        jnp.concatenate([partner, mine], axis_number),
        jnp.concatenate([mine, partner], axis_number),
    )


def halve_pick(current, upper_bit, axis_number):
    half_rows = current.shape[axis_number] // 2
    low_half = lax.slice_in_dim(current, 0, half_rows, axis=axis_number)
    high_half = lax.slice_in_dim(current, half_rows, 2 * half_rows, axis=axis_number)
    outgoing = jnp.where(upper_bit == 1, low_half, high_half)
    kept_half = jnp.where(upper_bit == 1, high_half, low_half)
    return (outgoing, kept_half)


def contract_last(left, right):
    return lax.dot_general(
        left, right, (((1,), (1,)), ((), ())), preferred_element_type=jnp.float32
    )


def general_device(hidden, w_qkv, w_out, segment_ids, end_positions, owners):
    devices = lax.axis_size("gx")
    blocks = devices // KVG
    group_bits = KVG.bit_length() - 1
    block_bits = blocks.bit_length() - 1
    my_index = lax.axis_index("gx")
    my_group = my_index % KVG
    my_block = my_index // KVG
    tokens = hidden.shape[0]
    query_width = HPG * HD
    block_rows = tokens // blocks
    scale = 1.0 / math.sqrt(HD)
    features = hidden
    for bit_number in range(group_bits):
        partner = from_partner(features, "gx", bit_number)
        features = join_pair(features, partner, my_group >> bit_number & 1, 1)
    partial_value = jnp.dot(features, w_qkv, preferred_element_type=jnp.float32)
    local_part = partial_value
    for level in reversed(range(block_bits)):
        outgoing, kept_half = halve_pick(local_part, my_block >> level & 1, 0)
        local_part = kept_half + from_partner(outgoing, "gx", group_bits + level)
    query_part = local_part[:, :query_width]
    pair_rows = local_part[:, query_width:].astype(jnp.bfloat16)
    for level in range(block_bits):
        partner = from_partner(pair_rows, "gx", group_bits + level)
        pair_rows = join_pair(pair_rows, partner, my_block >> level & 1, 0)
    key_block = pair_rows[:, :HD]
    value_block = pair_rows[:, HD:]
    queries = query_part.astype(jnp.bfloat16).reshape(block_rows * HPG, HD)
    start = my_block * block_rows
    my_segments = lax.dynamic_slice_in_dim(segment_ids, start, block_rows)
    row_segments = jnp.repeat(my_segments, HPG)
    row_positions = start + jnp.repeat(jnp.arange(block_rows, dtype=jnp.int32), HPG)
    positions = jnp.arange(tokens, dtype=jnp.int32)
    allowed = (row_segments[:, None] == segment_ids[None, :]) & (
        positions[None, :] <= row_positions[:, None]
    )
    scores, allowed = (contract_last(queries, key_block) * scale, allowed)
    row_max = jnp.max(jnp.where(allowed, scores, -jnp.inf), axis=1, keepdims=True)
    weights = jnp.where(allowed, jnp.exp(scores - row_max), 0.0)
    totals = jnp.sum(weights, axis=1, keepdims=True)
    mixed_heads = jnp.dot(
        weights.astype(jnp.bfloat16), value_block, preferred_element_type=jnp.float32
    )
    attended = (mixed_heads / totals).astype(jnp.bfloat16).reshape(block_rows, query_width)
    for level in range(block_bits):
        partner = from_partner(attended, "gx", group_bits + level)
        attended = join_pair(attended, partner, my_block >> level & 1, 0)
    output_part = contract_last(attended, w_out)
    for bit_number in reversed(range(group_bits)):
        outgoing, kept_half = halve_pick(output_part, my_group >> bit_number & 1, 1)
        output_part = kept_half + from_partner(outgoing, "gx", bit_number)
    mixed = output_part.astype(jnp.bfloat16)
    picker = (end_positions[:, None] == jnp.arange(tokens, dtype=jnp.int32)[None, :]).astype(
        jnp.bfloat16
    )
    end_local = jnp.dot(picker, mixed, preferred_element_type=jnp.float32).astype(jnp.bfloat16)
    end_full = lax.all_gather(end_local, "gx", axis=1, tiled=True)
    completions = owners.shape[0]
    same_owner = owners[:, None] == owners[None, :]
    earlier = jnp.arange(completions)[None, :] < jnp.arange(completions)[:, None]
    order_rank = jnp.sum((same_owner & earlier).astype(jnp.int32), axis=1)
    chooser = (
        (owners[None, :] == my_index)
        & (order_rank[None, :] == jnp.arange(SLOTS, dtype=jnp.int32)[:, None])
    ).astype(jnp.bfloat16)
    reward_rows = jnp.dot(chooser, end_full, preferred_element_type=jnp.float32).astype(
        jnp.bfloat16
    )
    return (mixed, reward_rows)


LANES = 128
ROW_PIECES = 3
ROW_TILE = 16
MIB = 1024 * 1024


def xor_swap(block, distance):
    count = lax.axis_size("gx")
    return lax.ppermute(block, "gx", [(low, low ^ distance) for low in range(count)])


def vmem():
    return pl.BlockSpec(memory_space=pltpu.VMEM)


def smem():
    return pl.BlockSpec(memory_space=pltpu.SMEM)


def anywhere():
    return pl.BlockSpec(memory_space=pl.ANY)


def project(features, distances, running, w_qkv, my_group, columns, first_column):
    tokens, width = features[0].shape
    count = len(features)
    piece = width // ROW_PIECES
    block_ids = jnp.stack([my_group ^ d for d in distances]).astype(jnp.int32)
    operands = list(features) + [w_qkv]
    if running is not None:
        operands.append(running)
    running_lanes = slice(0, columns)
    if running is not None and running.shape[1] > columns:
        running_lanes = slice(first_column, first_column + columns)

    def kernel(ids_ref, *refs):
        feature_refs = refs[:count]
        w_ref = refs[count]
        start_ref = refs[count + 1] if running is not None else None
        out_ref, current, slabs, sems = refs[-4:]

        def copy(block, part):
            rows = pl.ds(ids_ref[block] * width + part * piece, piece)
            return pltpu.make_async_copy(
                w_ref.at[rows, pl.ds(first_column, columns)], slabs.at[block, part], sems.at[block, part]
            )

        for block in range(count):
            for part in range(ROW_PIECES):
                copy(block, part).start()
        for block in range(count):
            current[block] = feature_refs[block][...]
        if start_ref is None:
            out_ref[...] = jnp.zeros_like(out_ref)
        else:
            out_ref[...] = start_ref[:, running_lanes]

        @pl.loop(0, count)
        def _(block):
            for part in range(ROW_PIECES):
                copy(block, part).wait()
                out_ref[...] += jnp.dot(
                    current[block, :, part * piece : (part + 1) * piece],
                    slabs[block, part],
                    preferred_element_type=jnp.float32,
                )

    return pl.pallas_call(
        kernel,
        in_specs=[smem()] + [vmem()] * count + [anywhere()] + ([] if running is None else [vmem()]),
        out_specs=vmem(),
        out_shape=jax.ShapeDtypeStruct((tokens, columns), jnp.float32),
        scratch_shapes=[
            pltpu.VMEM((count, tokens, width), jnp.bfloat16),
            pltpu.VMEM((count, ROW_PIECES, piece, columns), jnp.bfloat16),
            pltpu.SemaphoreType.DMA((count, ROW_PIECES)),
        ],
        compiler_params=pltpu.CompilerParams(vmem_limit_bytes=40 * MIB),
        cost_estimate=pl.CostEstimate(
            flops=2 * count * tokens * width * columns,
            bytes_accessed=2 * count * width * columns,
            transcendentals=0,
        ),
        name="project",
    )(block_ids, *operands)


def packed_tiles(tokens):
    blocks = tokens // ROW_TILE
    places = []
    for head in range(2):
        places.append((head, head, blocks - 1, 0))
        for low in range(blocks // 2 - 1):
            tile = 2 + head * (blocks // 2 - 1) + low
            places.append((tile, head, low, 0))
            places.append((tile, head, blocks - 2 - low, (low + 1) * ROW_TILE))
        places.append((blocks, head, blocks // 2 - 1, head * tokens // 2))
    return places


def partial_scores(queries, own_kv, partner_kv):
    tokens = queries.shape[0]
    blocks = tokens // ROW_TILE

    def kernel(query_ref, own_ref, partner_ref, value_ref, score_ref, packed_ref):
        pair = (own_ref[...] + partner_ref[...].astype(jnp.float32)).astype(jnp.bfloat16)
        keys = pair[:, :HD]
        value_ref[...] = pair[:, HD:]
        lane = lax.broadcasted_iota(jnp.int32, (ROW_TILE, tokens), 1)
        for first in range(0, HPG, 2):
            tiles = [None] * (blocks + 1)
            scores = []
            for head in range(first, first + 2):
                scores.append(
                    contract_last(query_ref[:, head * HD : (head + 1) * HD].astype(jnp.bfloat16), keys)
                )
                score_ref[head] = scores[-1]
            for tile, head, block, shift in packed_tiles(tokens):
                rows = scores[head][block * ROW_TILE : (block + 1) * ROW_TILE]
                if shift:
                    rows = jnp.where(lane < shift, tiles[tile], pltpu.roll(rows, shift, 1))
                tiles[tile] = rows
            for tile, rows in enumerate(tiles):
                packed_ref[first // 2, tile] = rows.astype(jnp.bfloat16)

    return pl.pallas_call(
        kernel,
        out_shape=[
            jax.ShapeDtypeStruct((tokens, HD), jnp.bfloat16),
            jax.ShapeDtypeStruct((HPG, tokens, tokens), jnp.float32),
            jax.ShapeDtypeStruct((HPG // 2, blocks + 1, ROW_TILE, tokens), jnp.bfloat16),
        ],
        compiler_params=pltpu.CompilerParams(vmem_limit_bytes=16 * MIB),
        cost_estimate=pl.CostEstimate(
            flops=2 * HPG * tokens * tokens * HD, bytes_accessed=2 * tokens * HPG * HD, transcendentals=0
        ),
        name="partial_scores",
    )(queries, own_kv, partner_kv)


def fetch_rows(block_ids, w_out, count):
    rows, columns = w_out.shape[0] // KVG, w_out.shape[1]

    def kernel(ids_ref, w_ref, *refs):
        out_refs, sems = refs[:-1], refs[-1]
        copies = [
            pltpu.make_async_copy(
                w_ref.at[pl.ds(ids_ref[block] * rows, rows)], out_refs[block // 2].at[block % 2], sems.at[block]
            )
            for block in range(count)
        ]
        for copy in copies:
            copy.start()
        for copy in copies:
            copy.wait()

    return pl.pallas_call(
        kernel,
        in_specs=[smem(), anywhere()],
        out_specs=[vmem()] * (count // 2),
        out_shape=[pltpu.VMEM((2, rows, columns), jnp.bfloat16)] * (count // 2),
        scratch_shapes=[pltpu.SemaphoreType.DMA((count,))],
        compiler_params=pltpu.CompilerParams(vmem_limit_bytes=2 * MIB),
        cost_estimate=pl.CostEstimate(
            flops=2 * count * LANES * rows * columns, bytes_accessed=2 * count * rows * columns, transcendentals=0
        ),
        name="fetch_rows",
    )(block_ids, w_out)


def mix_chip(attended, slab_ref, picker, even_ref, odd_ref, end_ref):
    for core, out_ref in enumerate((even_ref, odd_ref)):
        part = contract_last(attended[...], slab_ref[core]).astype(jnp.bfloat16)
        out_ref[...] = part
        end_ref[core] = jnp.dot(picker[...], part, preferred_element_type=jnp.float32)


def chip_shapes(tokens, rows, picker):
    part = jax.ShapeDtypeStruct((tokens, rows), jnp.bfloat16)
    return [part, part, jax.ShapeDtypeStruct((2, picker.shape[0], rows), jnp.float32)]


def attend_and_mix(own_scores, partner_scores, values, allowed, slabs, picker):
    heads, tokens = own_scores.shape[:2]
    blocks = tokens // ROW_TILE
    count, rows, columns = slabs.shape
    scale = 1.0 / math.sqrt(HD)

    def kernel(
        own_ref, partner_ref, value_ref, allowed_ref, slab_ref, picker_ref,
        attended_ref, even_ref, odd_ref, end_ref,
    ):
        mask = allowed_ref[...] > 0.0
        for two in range(heads // 2):
            partner = [[None] * blocks, [None] * blocks]
            for tile, head, block, shift in packed_tiles(tokens):
                rows_of = partner_ref[two, tile].astype(jnp.float32)
                partner[head][block] = pltpu.roll(rows_of, tokens - shift, 1) if shift else rows_of
            for core in range(2):
                head = 2 * two + core
                scores = (own_ref[head] + jnp.concatenate(partner[core], 0)) * scale
                row_max = jnp.max(jnp.where(mask, scores, -jnp.inf), axis=1, keepdims=True)
                weights = jnp.where(mask, jnp.exp(scores - row_max), 0.0)
                totals = jnp.sum(weights, axis=1, keepdims=True)
                mixed_heads = jnp.dot(
                    weights.astype(jnp.bfloat16), value_ref[...], preferred_element_type=jnp.float32
                )
                attended_ref[:, head * HD : (head + 1) * HD] = (mixed_heads / totals).astype(jnp.bfloat16)
        mix_chip(attended_ref, slab_ref, picker_ref, even_ref, odd_ref, end_ref)

    return pl.pallas_call(
        kernel,
        in_specs=[vmem()] * 6,
        out_specs=[vmem()] * 4,
        out_shape=[jax.ShapeDtypeStruct((tokens, columns), jnp.bfloat16)]
        + chip_shapes(tokens, rows, picker),
        compiler_params=pltpu.CompilerParams(vmem_limit_bytes=8 * MIB),
        cost_estimate=pl.CostEstimate(
            flops=4 * tokens * rows * columns,
            bytes_accessed=4 * rows * columns,
            transcendentals=heads * tokens * tokens,
        ),
        name="attend_and_mix",
    )(own_scores, partner_scores, values, allowed, slabs, picker)


def mix(attended, slabs, picker):
    tokens = attended.shape[0]
    rows, columns = slabs.shape[1:]

    def kernel(attended_ref, slab_ref, picker_ref, even_ref, odd_ref, end_ref):
        mix_chip(attended_ref, slab_ref, picker_ref, even_ref, odd_ref, end_ref)

    return pl.pallas_call(
        kernel,
        in_specs=[vmem()] * 3,
        out_specs=[vmem()] * 3,
        out_shape=chip_shapes(tokens, rows, picker),
        compiler_params=pltpu.CompilerParams(vmem_limit_bytes=8 * MIB),
        cost_estimate=pl.CostEstimate(flops=tokens * rows, bytes_accessed=rows, transcendentals=0),
        name="mix",
    )(attended, slabs, picker)


def add_rounded(left, right):
    return (left.astype(jnp.float32) + right.astype(jnp.float32)).astype(jnp.bfloat16)


def swap_blocks(blocks, distance):
    return [blocks[j ^ distance] for j in range(len(blocks))]


def natural_order(blocks, my_group):
    distance = 1
    while distance < len(blocks):
        bit = (my_group & distance) != 0
        swapped = swap_blocks(blocks, distance)
        blocks = [jnp.where(bit, other, own) for own, other in zip(blocks, swapped)]
        distance *= 2
    return jnp.concatenate(blocks, axis=-1)


def pair_device(hidden, w_qkv, w_out, segment_ids, end_positions, owners):
    my_index = lax.axis_index("gx")
    my_group = my_index % KVG
    my_block = my_index // KVG
    tokens = hidden.shape[0]
    query_width = HPG * HD
    together = lax.optimization_barrier
    positions = jnp.arange(tokens, dtype=jnp.int32)
    allowed = (
        (segment_ids[:, None] == segment_ids[None, :]) & (positions[None, :] <= positions[:, None])
    ).astype(jnp.float32)
    completions = owners.shape[0]
    end_rows = -(-completions // 8) * 8
    picker = (
        jnp.pad(end_positions, (0, end_rows - completions), constant_values=-1)[:, None] == positions[None, :]
    ).astype(jnp.bfloat16)
    same_owner = owners[:, None] == owners[None, :]
    earlier = jnp.arange(completions)[None, :] < jnp.arange(completions)[:, None]
    order_rank = jnp.sum((same_owner & earlier).astype(jnp.int32), axis=1)
    chooser = (
        (owners[None, :] == my_index)
        & (order_rank[None, :] == jnp.arange(SLOTS, dtype=jnp.int32)[:, None])
    ).astype(jnp.bfloat16)

    columns = w_qkv.shape[1]
    near_core = xor_swap(hidden, 1)
    from_y, from_z = xor_swap(hidden, 2), xor_swap(hidden, 4)
    early = project([hidden, near_core], (0, 1), None, w_qkv, my_group, columns, 0)
    from_y, from_z, sent, early = together((from_y, from_z, hidden, early))
    from_both = xor_swap(sent, 6)
    from_y_core, from_z_core = xor_swap(from_y, 1), xor_swap(from_z, 1)
    middle = project(
        [from_y, from_z, from_y_core, from_z_core], (2, 4, 3, 5), early, w_qkv, my_group, columns, 0
    )
    from_both, middle = together((from_both, middle))
    late = [from_both, xor_swap(from_both, 1)]
    own_kv = project(late, (6, 7), middle, w_qkv, my_group, 2 * HD, query_width)
    partner_kv = xor_swap(own_kv.astype(jnp.bfloat16), KVG)
    middle, own_kv = together((middle, own_kv))
    queries = project(late, (6, 7), middle, w_qkv, my_group, query_width, 0)

    values, scores, packed = partial_scores(queries, own_kv, partner_kv)
    block_ids = (my_group ^ jnp.arange(KVG, dtype=jnp.int32)).astype(jnp.int32)
    packed, block_ids = together((packed, block_ids))
    arrived = xor_swap(packed, KVG)
    own_slabs, slabs_y, slabs_z, slabs_both = fetch_rows(block_ids, w_out, KVG)
    arrived, slabs_both = together((arrived, slabs_both))
    attended, even_both, odd_both, ends_both = attend_and_mix(
        scores, arrived, values, allowed, slabs_both, picker
    )
    odd_both = xor_swap(odd_both, 1)
    even_y, odd_y, ends_y = mix(attended, slabs_y, picker)
    odd_both, even_y, odd_y = together((odd_both, even_y, odd_y))
    odd_y = xor_swap(odd_y, 1)
    near_both, attended = together((add_rounded(even_both, odd_both), attended))
    sum_both = xor_swap(near_both, 6)
    even_z, odd_z, ends_z = mix(attended, slabs_z, picker)
    odd_y, even_z, odd_z = together((odd_y, even_z, odd_z))
    odd_z = xor_swap(odd_z, 1)
    near_y, attended = together((add_rounded(even_y, odd_y), attended))
    sum_y = xor_swap(near_y, 2)
    even_own, odd_own, ends_own = mix(attended, own_slabs, picker)
    odd_z, even_own, odd_own, ends_own, sum_both = together((odd_z, even_own, odd_own, ends_own, sum_both))
    sum_z = xor_swap(add_rounded(even_z, odd_z), 4)

    end_parts = jnp.concatenate([ends_own, ends_y, ends_z, ends_both])[:, :completions]
    end_far = xor_swap(end_parts[1::2].astype(jnp.bfloat16), 1)
    ends = end_parts[0::2] + end_far.astype(jnp.float32)
    got = xor_swap(ends.astype(jnp.bfloat16), 2).astype(jnp.float32)
    odd_own = xor_swap(odd_own, 1)
    ends = [ends[i] + got[i ^ 1] for i in range(KVG // 2)]
    message = jnp.stack(ends).astype(jnp.bfloat16)
    got = xor_swap(message, 4).astype(jnp.float32)
    own_ends = jnp.stack([ends[i] + got[i ^ 2] for i in range(KVG // 2)]).astype(jnp.bfloat16)
    got = [xor_swap(message, KVG).astype(jnp.float32), xor_swap(message, KVG ^ 4).astype(jnp.float32)]
    other_ends = jnp.stack([got[0][i] + got[1][i ^ 2] for i in range(KVG // 2)]).astype(jnp.bfloat16)
    both = jnp.stack([own_ends, other_ends])
    both_far = xor_swap(both, 1)
    halves = []
    for half in range(2):
        blocks = []
        for i in range(KVG // 2):
            blocks += [both[half, i], both_far[half, i]]
        halves.append(natural_order(blocks, my_group))
    end_full = jnp.concatenate(
        [jnp.where(my_block == 0, halves[0], halves[1]), jnp.where(my_block == 0, halves[1], halves[0])], axis=-1
    )
    reward_rows = jnp.dot(chooser, end_full, preferred_element_type=jnp.float32).astype(jnp.bfloat16)

    mixed = even_own.astype(jnp.float32)
    for part in (odd_own, sum_y, sum_z, sum_both):
        mixed += part.astype(jnp.float32)
    return (mixed.astype(jnp.bfloat16), reward_rows)


def per_device(hidden, w_qkv, w_out, segment_ids, end_positions, owners):
    tokens, width = hidden.shape
    blocks = lax.axis_size("gx") // KVG
    if blocks == 2 and width % LANES == 0 and tokens == LANES:
        return pair_device(hidden, w_qkv, w_out, segment_ids, end_positions, owners)
    return general_device(hidden, w_qkv, w_out, segment_ids, end_positions, owners)


def solution(mesh):
    placed = (
        P("groups", "gx"),
        P("gx", None),
        P("gx", None),
        P("groups"),
        P("groups"),
        P("groups"),
    )
    return jax.shard_map(
        per_device,
        mesh=mesh,
        in_specs=placed,
        out_specs=(P("groups", "gx"), P(("groups", "gx"), None)),
        check_vma=False,
    )
```

```python
import math

import jax
import jax.numpy as jnp
from jax import lax
from jax.experimental import pallas as pl
from jax.experimental.pallas import tpu as pltpu
from jax.sharding import PartitionSpec as P

HD = 192
HPG = 12
KVG = 8
SLOTS = 2


def from_partner(block, axis, distance):
    count = lax.axis_size(axis)
    route = []
    for low in range(count):
        high = low | 1 << distance
        if high != low and high < count:
            route += [(low, high), (high, low)]
    return lax.ppermute(block, axis, route)


def join_pair(mine, partner, upper_bit, axis_number):
    return jnp.where(
        upper_bit == 1,
        jnp.concatenate([partner, mine], axis_number),
        jnp.concatenate([mine, partner], axis_number),
    )


def halve_pick(current, upper_bit, axis_number):
    half_rows = current.shape[axis_number] // 2
    low_half = lax.slice_in_dim(current, 0, half_rows, axis=axis_number)
    high_half = lax.slice_in_dim(current, half_rows, 2 * half_rows, axis=axis_number)
    outgoing = jnp.where(upper_bit == 1, low_half, high_half)
    kept_half = jnp.where(upper_bit == 1, high_half, low_half)
    return (outgoing, kept_half)


def contract_last(left, right):
    return lax.dot_general(
        left, right, (((1,), (1,)), ((), ())), preferred_element_type=jnp.float32
    )


def general_device(hidden, w_qkv, w_out, segment_ids, end_positions, owners):
    devices = lax.axis_size("gx")
    blocks = devices // KVG
    group_bits = KVG.bit_length() - 1
    block_bits = blocks.bit_length() - 1
    my_index = lax.axis_index("gx")
    my_group = my_index % KVG
    my_block = my_index // KVG
    tokens = hidden.shape[0]
    query_width = HPG * HD
    block_rows = tokens // blocks
    scale = 1.0 / math.sqrt(HD)
    features = hidden
    for bit_number in range(group_bits):
        partner = from_partner(features, "gx", bit_number)
        features = join_pair(features, partner, my_group >> bit_number & 1, 1)
    partial_value = jnp.dot(features, w_qkv, preferred_element_type=jnp.float32)
    local_part = partial_value
    for level in reversed(range(block_bits)):
        outgoing, kept_half = halve_pick(local_part, my_block >> level & 1, 0)
        local_part = kept_half + from_partner(outgoing, "gx", group_bits + level)
    query_part = local_part[:, :query_width]
    pair_rows = local_part[:, query_width:].astype(jnp.bfloat16)
    for level in range(block_bits):
        partner = from_partner(pair_rows, "gx", group_bits + level)
        pair_rows = join_pair(pair_rows, partner, my_block >> level & 1, 0)
    key_block = pair_rows[:, :HD]
    value_block = pair_rows[:, HD:]
    queries = query_part.astype(jnp.bfloat16).reshape(block_rows * HPG, HD)
    start = my_block * block_rows
    my_segments = lax.dynamic_slice_in_dim(segment_ids, start, block_rows)
    row_segments = jnp.repeat(my_segments, HPG)
    row_positions = start + jnp.repeat(jnp.arange(block_rows, dtype=jnp.int32), HPG)
    positions = jnp.arange(tokens, dtype=jnp.int32)
    allowed = (row_segments[:, None] == segment_ids[None, :]) & (
        positions[None, :] <= row_positions[:, None]
    )
    scores, allowed = (contract_last(queries, key_block) * scale, allowed)
    row_max = jnp.max(jnp.where(allowed, scores, -jnp.inf), axis=1, keepdims=True)
    weights = jnp.where(allowed, jnp.exp(scores - row_max), 0.0)
    totals = jnp.sum(weights, axis=1, keepdims=True)
    mixed_heads = jnp.dot(
        weights.astype(jnp.bfloat16), value_block, preferred_element_type=jnp.float32
    )
    attended = (mixed_heads / totals).astype(jnp.bfloat16).reshape(block_rows, query_width)
    for level in range(block_bits):
        partner = from_partner(attended, "gx", group_bits + level)
        attended = join_pair(attended, partner, my_block >> level & 1, 0)
    output_part = contract_last(attended, w_out)
    for bit_number in reversed(range(group_bits)):
        outgoing, kept_half = halve_pick(output_part, my_group >> bit_number & 1, 1)
        output_part = kept_half + from_partner(outgoing, "gx", bit_number)
    mixed = output_part.astype(jnp.bfloat16)
    picker = (end_positions[:, None] == jnp.arange(tokens, dtype=jnp.int32)[None, :]).astype(
        jnp.bfloat16
    )
    end_local = jnp.dot(picker, mixed, preferred_element_type=jnp.float32).astype(jnp.bfloat16)
    end_full = lax.all_gather(end_local, "gx", axis=1, tiled=True)
    completions = owners.shape[0]
    same_owner = owners[:, None] == owners[None, :]
    earlier = jnp.arange(completions)[None, :] < jnp.arange(completions)[:, None]
    order_rank = jnp.sum((same_owner & earlier).astype(jnp.int32), axis=1)
    chooser = (
        (owners[None, :] == my_index)
        & (order_rank[None, :] == jnp.arange(SLOTS, dtype=jnp.int32)[:, None])
    ).astype(jnp.bfloat16)
    reward_rows = jnp.dot(chooser, end_full, preferred_element_type=jnp.float32).astype(
        jnp.bfloat16
    )
    return (mixed, reward_rows)


LANES = 128
ROW_CUTS = (0, 384, 768, 1152)
ROW_TILE = 16
MIB = 1024 * 1024


def xor_swap(block, distance):
    count = lax.axis_size("gx")
    return lax.ppermute(block, "gx", [(low, low ^ distance) for low in range(count)])


def vmem():
    return pl.BlockSpec(memory_space=pltpu.VMEM)


def smem():
    return pl.BlockSpec(memory_space=pltpu.SMEM)


def anywhere():
    return pl.BlockSpec(memory_space=pl.ANY)


def project(features, distances, running, w_qkv, my_group, columns, first_column):
    tokens, width = features[0].shape
    count = len(features)
    cuts = [cut * width // ROW_CUTS[-1] for cut in ROW_CUTS]
    pieces = list(zip(cuts, cuts[1:]))
    block_ids = jnp.stack([my_group ^ d for d in distances]).astype(jnp.int32)
    operands = list(features) + [w_qkv]
    if running is not None:
        operands.append(running)
    running_lanes = slice(0, columns)
    if running is not None and running.shape[1] > columns:
        running_lanes = slice(first_column, first_column + columns)

    def kernel(ids_ref, *refs):
        feature_refs = refs[:count]
        w_ref = refs[count]
        start_ref = refs[count + 1] if running is not None else None
        out_ref, current, slabs, sems = refs[-4:]

        def copy(block, part):
            low, high = pieces[part]
            rows = pl.ds(ids_ref[block] * width + low, high - low)
            return pltpu.make_async_copy(
                w_ref.at[rows, pl.ds(first_column, columns)],
                slabs.at[block, pl.ds(low, high - low)],
                sems.at[block, part],
            )

        for block in range(count):
            for part in range(len(pieces)):
                copy(block, part).start()
        for block in range(count):
            current[block] = feature_refs[block][...]
        if start_ref is None:
            out_ref[...] = jnp.zeros_like(out_ref)
        else:
            out_ref[...] = start_ref[:, running_lanes]

        @pl.loop(0, count)
        def _(block):
            for part in range(len(pieces)):
                copy(block, part).wait()
                out_ref[...] += jnp.dot(
                    current[block, :, pieces[part][0] : pieces[part][1]],
                    slabs[block, pieces[part][0] : pieces[part][1]],
                    preferred_element_type=jnp.float32,
                )

    return pl.pallas_call(
        kernel,
        in_specs=[smem()]
        + [vmem()] * count
        + [anywhere()]
        + ([] if running is None else [vmem()]),
        out_specs=vmem(),
        out_shape=jax.ShapeDtypeStruct((tokens, columns), jnp.float32),
        scratch_shapes=[
            pltpu.VMEM((count, tokens, width), jnp.bfloat16),
            pltpu.VMEM((count, width, columns), jnp.bfloat16),
            pltpu.SemaphoreType.DMA((count, len(pieces))),
        ],
        compiler_params=pltpu.CompilerParams(
            vmem_limit_bytes=2 * count * width * (tokens + columns) + 2 * MIB
        ),
        cost_estimate=pl.CostEstimate(
            flops=2 * count * tokens * width * columns,
            bytes_accessed=2 * count * width * columns,
            transcendentals=0,
        ),
        name="project",
    )(block_ids, *operands)


def fetch_kv(block_ids, w_qkv, query_width):
    count, rows = block_ids.shape[0], w_qkv.shape[0] // KVG
    kv_width = w_qkv.shape[1] - query_width
    pieces = len(ROW_CUTS) - 1
    piece = rows // pieces

    def kernel(ids_ref, w_ref, kv_ref, sems):
        copies = [
            pltpu.make_async_copy(
                w_ref.at[pl.ds(ids_ref[block] * rows + part * piece, piece), pl.ds(query_width, kv_width)],
                kv_ref.at[block, pl.ds(part * piece, piece)],
                sems.at[block, part],
            )
            for block in range(count)
            for part in range(pieces)
        ]
        for copy in copies:
            copy.start()
        for copy in copies:
            copy.wait()

    return pl.pallas_call(
        kernel,
        in_specs=[smem(), anywhere()],
        out_specs=vmem(),
        out_shape=pltpu.VMEM((count, rows, kv_width), jnp.bfloat16),
        scratch_shapes=[pltpu.SemaphoreType.DMA((count, pieces))],
        compiler_params=pltpu.CompilerParams(vmem_limit_bytes=32 * MIB),
        cost_estimate=pl.CostEstimate(flops=rows, bytes_accessed=2 * rows * kv_width, transcendentals=0),
        name="fetch_kv",
    )(block_ids, w_qkv)


def fold_tokens(rows):
    half = rows.shape[0] // 2
    return jnp.concatenate([rows[:half], rows[half:]], 1)


def unfold_tokens(folded):
    width = folded.shape[1] // 2
    return jnp.concatenate([folded[:, :width], folded[:, width:]], 0)


def finish_kv(features, running, w_kv):
    tokens = running.shape[0]
    columns = w_kv.shape[2]
    first = running.shape[1] - columns

    def kernel(*refs):
        running_ref, w_ref, out_ref, key_ref = refs[-4:]
        total = running_ref[:, first:]
        for i, feature_ref in enumerate(refs[:-4]):
            total += jnp.dot(feature_ref[...], w_ref[i], preferred_element_type=jnp.float32)
        out_ref[...] = total
        key_ref[...] = fold_tokens(total[:, :HD]).astype(jnp.bfloat16)

    return pl.pallas_call(
        kernel,
        in_specs=[vmem()] * (len(features) + 2),
        out_specs=[vmem()] * 2,
        out_shape=[
            jax.ShapeDtypeStruct((tokens, columns), jnp.float32),
            jax.ShapeDtypeStruct((tokens // 2, columns), jnp.bfloat16),
        ],
        compiler_params=pltpu.CompilerParams(vmem_limit_bytes=8 * MIB),
        name="finish_kv",
    )(*features, running, w_kv)


def packed_tiles(tokens):
    blocks = tokens // ROW_TILE
    places = []
    for head in range(2):
        places.append((head, head, blocks - 1, 0))
        for low in range(blocks // 2 - 1):
            tile = 2 + head * (blocks // 2 - 1) + low
            places.append((tile, head, low, 0))
            places.append((tile, head, blocks - 2 - low, (low + 1) * ROW_TILE))
        places.append((blocks, head, blocks // 2 - 1, head * tokens // 2))
    return places


def value_tiles(tokens):
    return [
        (slice(row, row + ROW_TILE), slice(lane, lane + LANES))
        for row in range(0, tokens // 2, ROW_TILE)
        for lane in range(0, 2 * HD, LANES)
    ]


def partial_scores(queries, own_kv, partner_keys):
    tokens = queries.shape[0]
    blocks = tokens // ROW_TILE

    def kernel(query_ref, own_ref, partner_ref, score_ref, packed_ref):
        partner_keys = unfold_tokens(partner_ref[...].astype(jnp.float32))
        keys = (own_ref[:, :HD] + partner_keys).astype(jnp.bfloat16)
        lane = lax.broadcasted_iota(jnp.int32, (ROW_TILE, tokens), 1)
        for first in range(0, HPG, 2):
            tiles = [None] * (blocks + 1)
            scores = []
            for head in range(first, first + 2):
                scores.append(
                    contract_last(query_ref[:, head * HD : (head + 1) * HD].astype(jnp.bfloat16), keys)
                )
                score_ref[head] = scores[-1]
            for tile, head, block, shift in packed_tiles(tokens):
                rows = scores[head][block * ROW_TILE : (block + 1) * ROW_TILE]
                if shift:
                    rows = jnp.where(lane < shift, tiles[tile], pltpu.roll(rows, shift, 1))
                tiles[tile] = rows
            for tile, rows in enumerate(tiles):
                packed_ref[first // 2 * (blocks + 1) + tile] = rows.astype(jnp.bfloat16)
        folded = fold_tokens(own_ref[:, HD:])
        for tile, place in enumerate(value_tiles(tokens)):
            packed_ref[HPG // 2 * (blocks + 1) + tile] = folded[place].astype(jnp.bfloat16)

    return pl.pallas_call(
        kernel,
        out_shape=[
            jax.ShapeDtypeStruct((HPG, tokens, tokens), jnp.float32),
            jax.ShapeDtypeStruct(
                (HPG // 2 * (blocks + 1) + len(value_tiles(tokens)), ROW_TILE, tokens), jnp.bfloat16
            ),
        ],
        compiler_params=pltpu.CompilerParams(vmem_limit_bytes=16 * MIB),
        cost_estimate=pl.CostEstimate(
            flops=2 * HPG * tokens * tokens * HD, bytes_accessed=2 * tokens * HPG * HD, transcendentals=0
        ),
        name="partial_scores",
    )(queries, own_kv, partner_keys)


def fetch_rows(block_ids, w_out, count):
    rows, columns = w_out.shape[0] // KVG, w_out.shape[1]

    def kernel(ids_ref, w_ref, *refs):
        out_refs, sems = refs[:-1], refs[-1]
        copies = [
            pltpu.make_async_copy(
                w_ref.at[pl.ds(ids_ref[block] * rows, rows)], out_refs[block // 2].at[block % 2], sems.at[block]
            )
            for block in range(count)
        ]
        for copy in copies:
            copy.start()
        for copy in copies:
            copy.wait()

    return pl.pallas_call(
        kernel,
        in_specs=[smem(), anywhere()],
        out_specs=[vmem()] * (count // 2),
        out_shape=[pltpu.VMEM((2, rows, columns), jnp.bfloat16)] * (count // 2),
        scratch_shapes=[pltpu.SemaphoreType.DMA((count,))],
        compiler_params=pltpu.CompilerParams(vmem_limit_bytes=2 * MIB),
        cost_estimate=pl.CostEstimate(
            flops=2 * count * LANES * rows * columns, bytes_accessed=2 * count * rows * columns, transcendentals=0
        ),
        name="fetch_rows",
    )(block_ids, w_out)


def mix_chip(attended, slab_ref, even_ref, odd_ref, end_ref):
    tokens, end_rows = even_ref.shape[0], end_ref.shape[1]
    for core, out_ref in enumerate((even_ref, odd_ref)):
        part = contract_last(attended[...], slab_ref[core])
        out_ref[...] = part[:tokens].astype(jnp.bfloat16)
        end_ref[core] = part[tokens : tokens + end_rows]


def chip_shapes(tokens, rows, end_rows):
    part = jax.ShapeDtypeStruct((tokens, rows), jnp.bfloat16)
    return [part, part, jax.ShapeDtypeStruct((2, end_rows, rows), jnp.float32)]


def attend_and_mix(own_scores, partner_scores, own_kv, allowed, slabs, picker, end_rows):
    heads, tokens = own_scores.shape[:2]
    blocks = tokens // ROW_TILE
    count, rows, columns = slabs.shape
    scale = 1.0 / math.sqrt(HD)

    def kernel(
        own_ref, partner_ref, own_kv_ref, allowed_ref, slab_ref, picker_ref,
        attended_ref, even_ref, odd_ref, end_ref,
    ):
        mask = allowed_ref[...] > 0.0
        first_tile = heads // 2 * (blocks + 1)
        tiles = [partner_ref[first_tile + tile].astype(jnp.float32) for tile in range(len(value_tiles(tokens)))]
        across = 2 * HD // LANES
        folded = jnp.concatenate(
            [jnp.concatenate(tiles[i : i + across], 1) for i in range(0, len(tiles), across)], 0
        )
        value = (own_kv_ref[:, HD:] + unfold_tokens(folded)).astype(jnp.bfloat16)
        for two in range(heads // 2):
            partner = [[None] * blocks, [None] * blocks]
            for tile, head, block, shift in packed_tiles(tokens):
                rows_of = partner_ref[two * (blocks + 1) + tile].astype(jnp.float32)
                partner[head][block] = pltpu.roll(rows_of, tokens - shift, 1) if shift else rows_of
            for core in range(2):
                head = 2 * two + core
                scores = (own_ref[head] + jnp.concatenate(partner[core], 0)) * scale
                row_max = jnp.max(jnp.where(mask, scores, -jnp.inf), axis=1, keepdims=True)
                weights = jnp.where(mask, jnp.exp(scores - row_max), 0.0)
                totals = jnp.sum(weights, axis=1, keepdims=True)
                mixed_heads = jnp.dot(
                    weights.astype(jnp.bfloat16), value, preferred_element_type=jnp.float32
                )
                attended_ref[:tokens, head * HD : (head + 1) * HD] = (mixed_heads / totals).astype(jnp.bfloat16)
        attended_ref[tokens:] = jnp.dot(
            picker_ref[...], attended_ref[:tokens], preferred_element_type=jnp.float32
        ).astype(jnp.bfloat16)
        mix_chip(attended_ref, slab_ref, even_ref, odd_ref, end_ref)

    return pl.pallas_call(
        kernel,
        in_specs=[vmem()] * 6,
        out_specs=[vmem()] * 4,
        out_shape=[jax.ShapeDtypeStruct((tokens + picker.shape[0], columns), jnp.bfloat16)]
        + chip_shapes(tokens, rows, end_rows),
        compiler_params=pltpu.CompilerParams(vmem_limit_bytes=8 * MIB),
        cost_estimate=pl.CostEstimate(
            flops=4 * tokens * rows * columns,
            bytes_accessed=4 * rows * columns,
            transcendentals=heads * tokens * tokens,
        ),
        name="attend_and_mix",
    )(own_scores, partner_scores, own_kv, allowed, slabs, picker)


def mix(attended, slabs, tokens, end_rows):
    rows, columns = slabs.shape[1:]

    def kernel(attended_ref, slab_ref, even_ref, odd_ref, end_ref):
        mix_chip(attended_ref, slab_ref, even_ref, odd_ref, end_ref)

    return pl.pallas_call(
        kernel,
        in_specs=[vmem()] * 2,
        out_specs=[vmem()] * 3,
        out_shape=chip_shapes(tokens, rows, end_rows),
        compiler_params=pltpu.CompilerParams(vmem_limit_bytes=8 * MIB),
        cost_estimate=pl.CostEstimate(flops=tokens * rows, bytes_accessed=rows, transcendentals=0),
        name="mix",
    )(attended, slabs)


def add_rounded(left, right):
    return (left.astype(jnp.float32) + right.astype(jnp.float32)).astype(jnp.bfloat16)


def swap_blocks(blocks, distance):
    return [blocks[j ^ distance] for j in range(len(blocks))]


def natural_order(blocks, my_group):
    distance = 1
    while distance < len(blocks):
        bit = (my_group & distance) != 0
        swapped = swap_blocks(blocks, distance)
        blocks = [jnp.where(bit, other, own) for own, other in zip(blocks, swapped)]
        distance *= 2
    return jnp.concatenate(blocks, axis=-1)


def pair_device(hidden, w_qkv, w_out, segment_ids, end_positions, owners):
    my_index = lax.axis_index("gx")
    my_group = my_index % KVG
    my_block = my_index // KVG
    tokens = hidden.shape[0]
    query_width = HPG * HD
    together = lax.optimization_barrier
    completions = owners.shape[0]
    same_owner = owners[:, None] == owners[None, :]
    earlier = jnp.arange(completions)[None, :] < jnp.arange(completions)[:, None]
    order_rank = jnp.sum((same_owner & earlier).astype(jnp.int32), axis=1)
    chooser = (
        (owners[None, :] == my_index)
        & (order_rank[None, :] == jnp.arange(SLOTS, dtype=jnp.int32)[:, None])
    ).astype(jnp.bfloat16)

    columns = w_qkv.shape[1]
    near_core = xor_swap(hidden, 1)
    from_y, from_z = xor_swap(hidden, 2), xor_swap(hidden, 4)
    early = project([hidden, near_core], (0, 1), None, w_qkv, my_group, columns, 0)
    block_ids = (my_group ^ jnp.arange(KVG, dtype=jnp.int32)).astype(jnp.int32)
    from_y, from_z, sent, early = together((from_y, from_z, hidden, early))
    from_both = xor_swap(sent, 6)
    from_y_core, from_z_core = xor_swap(from_y, 1), xor_swap(from_z, 1)
    middle = project(
        [from_y, from_z, from_y_core, from_z_core], (2, 4, 3, 5), early, w_qkv, my_group, columns, 0
    )
    from_both, middle, block_ids, segment_ids, end_positions = together(
        (from_both, middle, block_ids, segment_ids, end_positions)
    )
    w_kv = fetch_kv(block_ids[KVG - 2 :], w_qkv, query_width)
    positions = jnp.arange(tokens, dtype=jnp.int32)
    allowed = (
        (segment_ids[:, None] == segment_ids[None, :]) & (positions[None, :] <= positions[:, None])
    ).astype(jnp.float32)
    end_rows = -(-completions // 8) * 8
    picked_rows = -(-completions // ROW_TILE) * ROW_TILE
    picker = (
        jnp.pad(end_positions, (0, picked_rows - completions), constant_values=-1)[:, None] == positions[None, :]
    ).astype(jnp.bfloat16)
    late = [from_both, xor_swap(from_both, 1)]
    own_kv, folded_keys = finish_kv(late, middle, w_kv)
    partner_keys = xor_swap(folded_keys, KVG)
    middle, own_kv = together((middle, own_kv))
    queries = project(late, (6, 7), middle, w_qkv, my_group, query_width, 0)

    scores, packed = partial_scores(queries, own_kv, partner_keys)
    packed, block_ids = together((packed, block_ids))
    arrived = xor_swap(packed, KVG)
    own_slabs, slabs_y, slabs_z, slabs_both = fetch_rows(block_ids, w_out, KVG)
    arrived, slabs_both = together((arrived, slabs_both))
    attended, even_both, odd_both, ends_both = attend_and_mix(
        scores, arrived, own_kv, allowed, slabs_both, picker, end_rows
    )
    odd_both = xor_swap(odd_both, 1)
    even_y, odd_y, ends_y = mix(attended, slabs_y, tokens, end_rows)
    odd_both, even_y, odd_y = together((odd_both, even_y, odd_y))
    odd_y = xor_swap(odd_y, 1)
    near_both, attended = together((add_rounded(even_both, odd_both), attended))
    sum_both = xor_swap(near_both, 6)
    even_z, odd_z, ends_z = mix(attended, slabs_z, tokens, end_rows)
    odd_y, even_z, odd_z = together((odd_y, even_z, odd_z))
    odd_z = xor_swap(odd_z, 1)
    near_y, attended = together((add_rounded(even_y, odd_y), attended))
    even_own, odd_own, ends_own = mix(attended, own_slabs, tokens, end_rows)
    odd_z, even_own, odd_own, ends_own, sum_both = together((odd_z, even_own, odd_own, ends_own, sum_both))
    near_z = add_rounded(even_z, odd_z)

    end_parts = jnp.concatenate([ends_own, ends_y, ends_z, ends_both])[:, :completions]
    end_far = xor_swap(end_parts[1::2].astype(jnp.bfloat16), 1)
    ends = end_parts[0::2] + end_far.astype(jnp.float32)
    ends, odd_own, near_y, near_z = together((ends, xor_swap(odd_own, 1), near_y, near_z))
    message = ends.astype(jnp.bfloat16)
    ends = [ends[i] for i in range(KVG // 2)]
    for distance in range(2, KVG, 2):
        got = xor_swap(message, distance).astype(jnp.float32)
        ends = [ends[i] + got[i ^ distance // 2] for i in range(KVG // 2)]
    sum_y, sum_z = xor_swap(near_y, 2), xor_swap(near_z, 4)
    ends = jnp.stack(ends).astype(jnp.bfloat16)
    both = jnp.stack([ends, xor_swap(ends, KVG)])
    both, sum_y, sum_z = together((both, sum_y, sum_z))
    both_far = xor_swap(both, 1)
    halves = []
    for half in range(2):
        blocks = []
        for i in range(KVG // 2):
            blocks += [both[half, i], both_far[half, i]]
        halves.append(natural_order(blocks, my_group))
    end_full = jnp.concatenate(
        [jnp.where(my_block == 0, halves[0], halves[1]), jnp.where(my_block == 0, halves[1], halves[0])], axis=-1
    )
    reward_rows = jnp.dot(chooser, end_full, preferred_element_type=jnp.float32).astype(jnp.bfloat16)

    mixed = even_own.astype(jnp.float32)
    for part in (odd_own, sum_y, sum_z, sum_both):
        mixed += part.astype(jnp.float32)
    return (mixed.astype(jnp.bfloat16), reward_rows)


def per_device(hidden, w_qkv, w_out, segment_ids, end_positions, owners):
    tokens, width = hidden.shape
    blocks = lax.axis_size("gx") // KVG
    if blocks == 2 and width % LANES == 0 and tokens == LANES:
        return pair_device(hidden, w_qkv, w_out, segment_ids, end_positions, owners)
    return general_device(hidden, w_qkv, w_out, segment_ids, end_positions, owners)


def solution(mesh):
    placed = (
        P("groups", "gx"),
        P("gx", None),
        P("gx", None),
        P("groups"),
        P("groups"),
        P("groups"),
    )
    return jax.shard_map(
        per_device,
        mesh=mesh,
        in_specs=placed,
        out_specs=(P("groups", "gx"), P(("groups", "gx"), None)),
        check_vma=False,
    )
```

```python
import math

import jax
import jax.numpy as jnp
from jax import lax
from jax.experimental import pallas as pl
from jax.experimental.pallas import tpu as pltpu
from jax.sharding import PartitionSpec as P

HD = 192
HPG = 12
KVG = 8
SLOTS = 2


def from_partner(block, axis, distance):
    count = lax.axis_size(axis)
    route = []
    for low in range(count):
        high = low | 1 << distance
        if high != low and high < count:
            route += [(low, high), (high, low)]
    return lax.ppermute(block, axis, route)


def join_pair(mine, partner, upper_bit, axis_number):
    return jnp.where(
        upper_bit == 1,
        jnp.concatenate([partner, mine], axis_number),
        jnp.concatenate([mine, partner], axis_number),
    )


def halve_pick(current, upper_bit, axis_number):
    half_rows = current.shape[axis_number] // 2
    low_half = lax.slice_in_dim(current, 0, half_rows, axis=axis_number)
    high_half = lax.slice_in_dim(current, half_rows, 2 * half_rows, axis=axis_number)
    outgoing = jnp.where(upper_bit == 1, low_half, high_half)
    kept_half = jnp.where(upper_bit == 1, high_half, low_half)
    return (outgoing, kept_half)


def contract_last(left, right):
    return lax.dot_general(
        left, right, (((1,), (1,)), ((), ())), preferred_element_type=jnp.float32
    )


def general_device(hidden, w_qkv, w_out, segment_ids, end_positions, owners):
    devices = lax.axis_size("gx")
    blocks = devices // KVG
    group_bits = KVG.bit_length() - 1
    block_bits = blocks.bit_length() - 1
    my_index = lax.axis_index("gx")
    my_group = my_index % KVG
    my_block = my_index // KVG
    tokens = hidden.shape[0]
    query_width = HPG * HD
    block_rows = tokens // blocks
    scale = 1.0 / math.sqrt(HD)
    features = hidden
    for bit_number in range(group_bits):
        partner = from_partner(features, "gx", bit_number)
        features = join_pair(features, partner, my_group >> bit_number & 1, 1)
    partial_value = jnp.dot(features, w_qkv, preferred_element_type=jnp.float32)
    local_part = partial_value
    for level in reversed(range(block_bits)):
        outgoing, kept_half = halve_pick(local_part, my_block >> level & 1, 0)
        local_part = kept_half + from_partner(outgoing, "gx", group_bits + level)
    query_part = local_part[:, :query_width]
    pair_rows = local_part[:, query_width:].astype(jnp.bfloat16)
    for level in range(block_bits):
        partner = from_partner(pair_rows, "gx", group_bits + level)
        pair_rows = join_pair(pair_rows, partner, my_block >> level & 1, 0)
    key_block = pair_rows[:, :HD]
    value_block = pair_rows[:, HD:]
    queries = query_part.astype(jnp.bfloat16).reshape(block_rows * HPG, HD)
    start = my_block * block_rows
    my_segments = lax.dynamic_slice_in_dim(segment_ids, start, block_rows)
    row_segments = jnp.repeat(my_segments, HPG)
    row_positions = start + jnp.repeat(jnp.arange(block_rows, dtype=jnp.int32), HPG)
    positions = jnp.arange(tokens, dtype=jnp.int32)
    allowed = (row_segments[:, None] == segment_ids[None, :]) & (
        positions[None, :] <= row_positions[:, None]
    )
    scores, allowed = (contract_last(queries, key_block) * scale, allowed)
    row_max = jnp.max(jnp.where(allowed, scores, -jnp.inf), axis=1, keepdims=True)
    weights = jnp.where(allowed, jnp.exp(scores - row_max), 0.0)
    totals = jnp.sum(weights, axis=1, keepdims=True)
    mixed_heads = jnp.dot(
        weights.astype(jnp.bfloat16), value_block, preferred_element_type=jnp.float32
    )
    attended = (mixed_heads / totals).astype(jnp.bfloat16).reshape(block_rows, query_width)
    for level in range(block_bits):
        partner = from_partner(attended, "gx", group_bits + level)
        attended = join_pair(attended, partner, my_block >> level & 1, 0)
    output_part = contract_last(attended, w_out)
    for bit_number in reversed(range(group_bits)):
        outgoing, kept_half = halve_pick(output_part, my_group >> bit_number & 1, 1)
        output_part = kept_half + from_partner(outgoing, "gx", bit_number)
    mixed = output_part.astype(jnp.bfloat16)
    picker = (end_positions[:, None] == jnp.arange(tokens, dtype=jnp.int32)[None, :]).astype(
        jnp.bfloat16
    )
    end_local = jnp.dot(picker, mixed, preferred_element_type=jnp.float32).astype(jnp.bfloat16)
    end_full = lax.all_gather(end_local, "gx", axis=1, tiled=True)
    completions = owners.shape[0]
    same_owner = owners[:, None] == owners[None, :]
    earlier = jnp.arange(completions)[None, :] < jnp.arange(completions)[:, None]
    order_rank = jnp.sum((same_owner & earlier).astype(jnp.int32), axis=1)
    chooser = (
        (owners[None, :] == my_index)
        & (order_rank[None, :] == jnp.arange(SLOTS, dtype=jnp.int32)[:, None])
    ).astype(jnp.bfloat16)
    reward_rows = jnp.dot(chooser, end_full, preferred_element_type=jnp.float32).astype(
        jnp.bfloat16
    )
    return (mixed, reward_rows)


LANES = 128
ROW_CUTS = (0, 384, 768, 1152)
ROW_TILE = 16
MIB = 1024 * 1024


def xor_swap(block, distance):
    count = lax.axis_size("gx")
    return lax.ppermute(block, "gx", [(low, low ^ distance) for low in range(count)])


def vmem():
    return pl.BlockSpec(memory_space=pltpu.VMEM)


def smem():
    return pl.BlockSpec(memory_space=pltpu.SMEM)


def anywhere():
    return pl.BlockSpec(memory_space=pl.ANY)


def project(features, distances, running, w_qkv, my_group, columns, first_column):
    tokens, width = features[0].shape
    count = len(features)
    cuts = [cut * width // ROW_CUTS[-1] for cut in ROW_CUTS]
    pieces = list(zip(cuts, cuts[1:]))
    block_ids = jnp.stack([my_group ^ d for d in distances]).astype(jnp.int32)
    operands = list(features) + [w_qkv]
    if running is not None:
        operands.append(running)
    running_lanes = slice(0, columns)
    if running is not None and running.shape[1] > columns:
        running_lanes = slice(first_column, first_column + columns)

    def kernel(ids_ref, *refs):
        feature_refs = refs[:count]
        w_ref = refs[count]
        start_ref = refs[count + 1] if running is not None else None
        out_ref, current, slabs, sems = refs[-4:]

        def copy(block, part):
            low, high = pieces[part]
            rows = pl.ds(ids_ref[block] * width + low, high - low)
            return pltpu.make_async_copy(
                w_ref.at[rows, pl.ds(first_column, columns)],
                slabs.at[block, pl.ds(low, high - low)],
                sems.at[block, part],
            )

        for block in range(count):
            for part in range(len(pieces)):
                copy(block, part).start()
        for block in range(count):
            current[block] = feature_refs[block][...]
        if start_ref is None:
            out_ref[...] = jnp.zeros_like(out_ref)
        else:
            out_ref[...] = start_ref[:, running_lanes]

        @pl.loop(0, count)
        def _(block):
            for part in range(len(pieces)):
                copy(block, part).wait()
                out_ref[...] += jnp.dot(
                    current[block, :, pieces[part][0] : pieces[part][1]],
                    slabs[block, pieces[part][0] : pieces[part][1]],
                    preferred_element_type=jnp.float32,
                )

    return pl.pallas_call(
        kernel,
        in_specs=[smem()]
        + [vmem()] * count
        + [anywhere()]
        + ([] if running is None else [vmem()]),
        out_specs=vmem(),
        out_shape=jax.ShapeDtypeStruct((tokens, columns), jnp.float32),
        scratch_shapes=[
            pltpu.VMEM((count, tokens, width), jnp.bfloat16),
            pltpu.VMEM((count, width, columns), jnp.bfloat16),
            pltpu.SemaphoreType.DMA((count, len(pieces))),
        ],
        compiler_params=pltpu.CompilerParams(
            vmem_limit_bytes=2 * count * width * (tokens + columns) + 2 * MIB
        ),
        cost_estimate=pl.CostEstimate(
            flops=2 * count * tokens * width * columns,
            bytes_accessed=2 * count * width * columns,
            transcendentals=0,
        ),
        name="project",
    )(block_ids, *operands)


def fetch_kv(block_ids, w_qkv, query_width):
    count, rows = block_ids.shape[0], w_qkv.shape[0] // KVG
    kv_width = w_qkv.shape[1] - query_width
    pieces = len(ROW_CUTS) - 1
    piece = rows // pieces

    def kernel(ids_ref, w_ref, kv_ref, sems):
        copies = [
            pltpu.make_async_copy(
                w_ref.at[pl.ds(ids_ref[block] * rows + part * piece, piece), pl.ds(query_width, kv_width)],
                kv_ref.at[block, pl.ds(part * piece, piece)],
                sems.at[block, part],
            )
            for block in range(count)
            for part in range(pieces)
        ]
        for copy in copies:
            copy.start()
        for copy in copies:
            copy.wait()

    return pl.pallas_call(
        kernel,
        in_specs=[smem(), anywhere()],
        out_specs=vmem(),
        out_shape=pltpu.VMEM((count, rows, kv_width), jnp.bfloat16),
        scratch_shapes=[pltpu.SemaphoreType.DMA((count, pieces))],
        compiler_params=pltpu.CompilerParams(vmem_limit_bytes=32 * MIB),
        cost_estimate=pl.CostEstimate(flops=rows, bytes_accessed=2 * rows * kv_width, transcendentals=0),
        name="fetch_kv",
    )(block_ids, w_qkv)


def fold_tokens(rows):
    half = rows.shape[0] // 2
    return jnp.concatenate([rows[:half], rows[half:]], 1)


def unfold_tokens(folded):
    width = folded.shape[1] // 2
    return jnp.concatenate([folded[:, :width], folded[:, width:]], 0)


def finish_kv(features, running, w_kv):
    tokens = running.shape[0]
    columns = w_kv.shape[2]
    first = running.shape[1] - columns

    def kernel(*refs):
        running_ref, w_ref, out_ref, key_ref = refs[-4:]
        total = running_ref[:, first:]
        for i, feature_ref in enumerate(refs[:-4]):
            total += jnp.dot(feature_ref[...], w_ref[i], preferred_element_type=jnp.float32)
        out_ref[...] = total
        key_ref[...] = fold_tokens(total[:, :HD]).astype(jnp.bfloat16)

    return pl.pallas_call(
        kernel,
        in_specs=[vmem()] * (len(features) + 2),
        out_specs=[vmem()] * 2,
        out_shape=[
            jax.ShapeDtypeStruct((tokens, columns), jnp.float32),
            jax.ShapeDtypeStruct((tokens // 2, columns), jnp.bfloat16),
        ],
        compiler_params=pltpu.CompilerParams(vmem_limit_bytes=8 * MIB),
        name="finish_kv",
    )(*features, running, w_kv)


def packed_tiles(tokens):
    blocks = tokens // ROW_TILE
    places = []
    for head in range(2):
        places.append((head, head, blocks - 1, 0))
        for low in range(blocks // 2 - 1):
            tile = 2 + head * (blocks // 2 - 1) + low
            places.append((tile, head, low, 0))
            places.append((tile, head, blocks - 2 - low, (low + 1) * ROW_TILE))
        places.append((blocks, head, blocks // 2 - 1, head * tokens // 2))
    return places


def value_tiles(tokens):
    return [
        (slice(row, row + ROW_TILE), slice(lane, lane + LANES))
        for row in range(0, tokens // 2, ROW_TILE)
        for lane in range(0, 2 * HD, LANES)
    ]


def partial_scores(queries, own_kv, partner_keys):
    tokens = queries.shape[0]
    blocks = tokens // ROW_TILE

    def kernel(query_ref, own_ref, partner_ref, score_ref, packed_ref):
        partner_keys = unfold_tokens(partner_ref[...].astype(jnp.float32))
        keys = (own_ref[:, :HD] + partner_keys).astype(jnp.bfloat16)
        lane = lax.broadcasted_iota(jnp.int32, (ROW_TILE, tokens), 1)
        for first in range(0, HPG, 2):
            tiles = [None] * (blocks + 1)
            scores = []
            for head in range(first, first + 2):
                scores.append(
                    contract_last(query_ref[:, head * HD : (head + 1) * HD].astype(jnp.bfloat16), keys)
                )
                score_ref[head] = scores[-1]
            for tile, head, block, shift in packed_tiles(tokens):
                rows = scores[head][block * ROW_TILE : (block + 1) * ROW_TILE]
                if shift:
                    rows = jnp.where(lane < shift, tiles[tile], pltpu.roll(rows, shift, 1))
                tiles[tile] = rows
            for tile, rows in enumerate(tiles):
                packed_ref[first // 2 * (blocks + 1) + tile] = rows.astype(jnp.bfloat16)
        folded = fold_tokens(own_ref[:, HD:])
        for tile, place in enumerate(value_tiles(tokens)):
            packed_ref[HPG // 2 * (blocks + 1) + tile] = folded[place].astype(jnp.bfloat16)

    return pl.pallas_call(
        kernel,
        out_shape=[
            jax.ShapeDtypeStruct((HPG, tokens, tokens), jnp.float32),
            jax.ShapeDtypeStruct(
                (HPG // 2 * (blocks + 1) + len(value_tiles(tokens)), ROW_TILE, tokens), jnp.bfloat16
            ),
        ],
        compiler_params=pltpu.CompilerParams(vmem_limit_bytes=16 * MIB),
        cost_estimate=pl.CostEstimate(
            flops=2 * HPG * tokens * tokens * HD, bytes_accessed=2 * tokens * HPG * HD, transcendentals=0
        ),
        name="partial_scores",
    )(queries, own_kv, partner_keys)


def fetch_rows(block_ids, w_out, count):
    rows, columns = w_out.shape[0] // KVG, w_out.shape[1]

    def kernel(ids_ref, w_ref, *refs):
        out_refs, sems = refs[:-1], refs[-1]
        copies = [
            pltpu.make_async_copy(
                w_ref.at[pl.ds(ids_ref[block] * rows, rows)], out_refs[block // 2].at[block % 2], sems.at[block]
            )
            for block in range(count)
        ]
        for copy in copies:
            copy.start()
        for copy in copies:
            copy.wait()

    return pl.pallas_call(
        kernel,
        in_specs=[smem(), anywhere()],
        out_specs=[vmem()] * (count // 2),
        out_shape=[pltpu.VMEM((2, rows, columns), jnp.bfloat16)] * (count // 2),
        scratch_shapes=[pltpu.SemaphoreType.DMA((count,))],
        compiler_params=pltpu.CompilerParams(vmem_limit_bytes=2 * MIB),
        cost_estimate=pl.CostEstimate(
            flops=2 * count * LANES * rows * columns, bytes_accessed=2 * count * rows * columns, transcendentals=0
        ),
        name="fetch_rows",
    )(block_ids, w_out)


def mix_chip(attended, slab_ref, even_ref, odd_ref):
    for core, out_ref in enumerate((even_ref, odd_ref)):
        out_ref[...] = contract_last(attended[...], slab_ref[core]).astype(jnp.bfloat16)


def attend_and_mix(own_scores, partner_scores, own_kv, allowed, slabs, picker):
    heads, tokens = own_scores.shape[:2]
    blocks = tokens // ROW_TILE
    count, rows, columns = slabs.shape
    scale = 1.0 / math.sqrt(HD)

    def kernel(
        own_ref, partner_ref, own_kv_ref, allowed_ref, slab_ref, picker_ref,
        attended_ref, even_ref, odd_ref,
    ):
        mask = allowed_ref[...] > 0.0
        first_tile = heads // 2 * (blocks + 1)
        tiles = [partner_ref[first_tile + tile].astype(jnp.float32) for tile in range(len(value_tiles(tokens)))]
        across = 2 * HD // LANES
        folded = jnp.concatenate(
            [jnp.concatenate(tiles[i : i + across], 1) for i in range(0, len(tiles), across)], 0
        )
        value = (own_kv_ref[:, HD:] + unfold_tokens(folded)).astype(jnp.bfloat16)
        for two in range(heads // 2):
            partner = [[None] * blocks, [None] * blocks]
            for tile, head, block, shift in packed_tiles(tokens):
                rows_of = partner_ref[two * (blocks + 1) + tile].astype(jnp.float32)
                partner[head][block] = pltpu.roll(rows_of, tokens - shift, 1) if shift else rows_of
            for core in range(2):
                head = 2 * two + core
                scores = (own_ref[head] + jnp.concatenate(partner[core], 0)) * scale
                row_max = jnp.max(jnp.where(mask, scores, -jnp.inf), axis=1, keepdims=True)
                weights = jnp.where(mask, jnp.exp(scores - row_max), 0.0)
                totals = jnp.sum(weights, axis=1, keepdims=True)
                mixed_heads = jnp.dot(
                    weights.astype(jnp.bfloat16), value, preferred_element_type=jnp.float32
                )
                attended_ref[:tokens, head * HD : (head + 1) * HD] = (mixed_heads / totals).astype(jnp.bfloat16)
        attended_ref[tokens:] = jnp.dot(
            picker_ref[...], attended_ref[:tokens], preferred_element_type=jnp.float32
        ).astype(jnp.bfloat16)
        mix_chip(attended_ref, slab_ref, even_ref, odd_ref)

    out_rows = tokens + picker.shape[0]
    return pl.pallas_call(
        kernel,
        in_specs=[vmem()] * 6,
        out_specs=[vmem()] * 3,
        out_shape=[jax.ShapeDtypeStruct((out_rows, columns), jnp.bfloat16)]
        + [jax.ShapeDtypeStruct((out_rows, rows), jnp.bfloat16)] * 2,
        compiler_params=pltpu.CompilerParams(vmem_limit_bytes=8 * MIB),
        cost_estimate=pl.CostEstimate(
            flops=4 * tokens * rows * columns,
            bytes_accessed=4 * rows * columns,
            transcendentals=heads * tokens * tokens,
        ),
        name="attend_and_mix",
    )(own_scores, partner_scores, own_kv, allowed, slabs, picker)


def mix(attended, slabs):
    out_rows = attended.shape[0]
    rows = slabs.shape[1]

    def kernel(attended_ref, slab_ref, even_ref, odd_ref):
        mix_chip(attended_ref, slab_ref, even_ref, odd_ref)

    return pl.pallas_call(
        kernel,
        in_specs=[vmem()] * 2,
        out_specs=[vmem()] * 2,
        out_shape=[jax.ShapeDtypeStruct((out_rows, rows), jnp.bfloat16)] * 2,
        compiler_params=pltpu.CompilerParams(vmem_limit_bytes=8 * MIB),
        cost_estimate=pl.CostEstimate(flops=out_rows * rows, bytes_accessed=rows, transcendentals=0),
        name="mix",
    )(attended, slabs)


def place_rewards(chooser, positions, blocks):
    slots = SLOTS
    places = chooser.shape[0] // slots
    features = blocks[0].shape[1]

    def kernel(chooser_ref, position_ref, *refs):
        out_ref = refs[-1]
        for i, block_ref in enumerate(refs[:-1]):
            chosen = jnp.dot(chooser_ref[...], block_ref[...], preferred_element_type=jnp.float32)
            for place in range(places):
                lanes = pl.ds(pl.multiple_of(position_ref[i * places + place] * features, LANES), features)
                out_ref[:, lanes] = chosen[place * slots : (place + 1) * slots].astype(jnp.bfloat16)

    return pl.pallas_call(
        kernel,
        in_specs=[vmem(), smem()] + [vmem()] * len(blocks),
        out_specs=vmem(),
        out_shape=jax.ShapeDtypeStruct((slots, len(blocks) * places * features), jnp.bfloat16),
        compiler_params=pltpu.CompilerParams(vmem_limit_bytes=8 * MIB),
        name="place_rewards",
    )(chooser, positions, *blocks)


def swap_groups(rows, groups, distance):
    size = rows.shape[0] // groups
    return jnp.concatenate([rows[(j ^ distance) * size : ((j ^ distance) + 1) * size] for j in range(groups)], 0)


def add_rounded(left, right):
    return (left.astype(jnp.float32) + right.astype(jnp.float32)).astype(jnp.bfloat16)


def pair_device(hidden, w_qkv, w_out, segment_ids, end_positions, owners):
    my_index = lax.axis_index("gx")
    my_group = my_index % KVG
    tokens = hidden.shape[0]
    query_width = HPG * HD
    together = lax.optimization_barrier
    completions = owners.shape[0]
    same_owner = owners[:, None] == owners[None, :]
    earlier = jnp.arange(completions)[None, :] < jnp.arange(completions)[:, None]
    order_rank = jnp.sum((same_owner & earlier).astype(jnp.int32), axis=1)
    chooser = (
        (owners[None, :] == my_index)
        & (order_rank[None, :] == jnp.arange(SLOTS, dtype=jnp.int32)[:, None])
    ).astype(jnp.bfloat16)

    columns = w_qkv.shape[1]
    near_core = xor_swap(hidden, 1)
    from_y, from_z = xor_swap(hidden, 2), xor_swap(hidden, 4)
    early = project([hidden, near_core], (0, 1), None, w_qkv, my_group, columns, 0)
    block_ids = (my_group ^ jnp.arange(KVG, dtype=jnp.int32)).astype(jnp.int32)
    from_y, from_z, sent, early = together((from_y, from_z, hidden, early))
    from_both = xor_swap(sent, 6)
    from_y_core, from_z_core = xor_swap(from_y, 1), xor_swap(from_z, 1)
    middle = project(
        [from_y, from_z, from_y_core, from_z_core], (2, 4, 3, 5), early, w_qkv, my_group, columns, 0
    )
    from_both, middle, block_ids, segment_ids, end_positions = together(
        (from_both, middle, block_ids, segment_ids, end_positions)
    )
    w_kv = fetch_kv(block_ids[KVG - 2 :], w_qkv, query_width)
    positions = jnp.arange(tokens, dtype=jnp.int32)
    allowed = (
        (segment_ids[:, None] == segment_ids[None, :]) & (positions[None, :] <= positions[:, None])
    ).astype(jnp.float32)
    picked_rows = -(-completions // ROW_TILE) * ROW_TILE
    picker = (
        jnp.pad(end_positions, (0, picked_rows - completions), constant_values=-1)[:, None] == positions[None, :]
    ).astype(jnp.bfloat16)
    late = [from_both, xor_swap(from_both, 1)]
    own_kv, folded_keys = finish_kv(late, middle, w_kv)
    partner_keys = xor_swap(folded_keys, KVG)
    middle, own_kv = together((middle, own_kv))
    queries = project(late, (6, 7), middle, w_qkv, my_group, query_width, 0)

    scores, packed = partial_scores(queries, own_kv, partner_keys)
    packed, block_ids = together((packed, block_ids))
    arrived = xor_swap(packed, KVG)
    own_slabs, slabs_y, slabs_z, slabs_both = fetch_rows(block_ids, w_out, KVG)
    arrived, slabs_both = together((arrived, slabs_both))
    attended, even_both, odd_both = attend_and_mix(scores, arrived, own_kv, allowed, slabs_both, picker)
    odd_both = xor_swap(odd_both, 1)
    even_y, odd_y = mix(attended, slabs_y)
    odd_both, even_y, odd_y = together((odd_both, even_y, odd_y))
    odd_y = xor_swap(odd_y, 1)
    near_both, attended = together((add_rounded(even_both[:tokens], odd_both[:tokens]), attended))
    sum_both = xor_swap(near_both, 6)
    even_z, odd_z = mix(attended, slabs_z)
    odd_y, even_z, odd_z = together((odd_y, even_z, odd_z))
    odd_z = xor_swap(odd_z, 1)
    near_y, attended = together((add_rounded(even_y[:tokens], odd_y[:tokens]), attended))
    even_own, odd_own = mix(attended, own_slabs)
    odd_z, even_own, odd_own = together((odd_z, even_own, odd_own))
    odd_own = xor_swap(odd_own, 1)
    near_z = add_rounded(even_z[:tokens], odd_z[:tokens])

    ends = jnp.concatenate(
        [
            even[tokens : tokens + completions].astype(jnp.float32)
            + odd[tokens : tokens + completions].astype(jnp.float32)
            for even, odd in ((even_own, odd_own), (even_y, odd_y), (even_z, odd_z), (even_both, odd_both))
        ]
    )
    ends, near_y, near_z, sum_both = together((ends, near_y, near_z, sum_both))
    message = ends.astype(jnp.bfloat16)
    for distance in range(2, KVG, 2):
        got = xor_swap(message, distance).astype(jnp.float32)
        ends += swap_groups(got, KVG // 2, distance // 2)
    sum_z, sum_y = xor_swap(near_z, 4), xor_swap(near_y, 2)
    ends = ends.astype(jnp.bfloat16)
    other_ends = xor_swap(ends, KVG)
    both, sum_z, sum_y = together((jnp.concatenate([ends, other_ends]), sum_z, sum_y))
    both_far = xor_swap(both, 1)
    chips = 2 * jnp.arange(KVG // 2, dtype=jnp.int32)
    halves = KVG * jnp.arange(2, dtype=jnp.int32)
    distances = (halves[:, None] + chips[None, :]).reshape(-1)
    places = my_index ^ jnp.concatenate([distances, distances + 1])
    reward_rows = place_rewards(jnp.kron(jnp.eye(KVG, dtype=jnp.bfloat16), chooser), places.astype(jnp.int32), [both, both_far])

    mixed = even_own[:tokens].astype(jnp.float32)
    for part in (odd_own[:tokens], sum_y, sum_z, sum_both):
        mixed += part.astype(jnp.float32)
    return (mixed.astype(jnp.bfloat16), reward_rows)


def per_device(hidden, w_qkv, w_out, segment_ids, end_positions, owners):
    tokens, width = hidden.shape
    blocks = lax.axis_size("gx") // KVG
    if blocks == 2 and width % LANES == 0 and tokens == LANES:
        return pair_device(hidden, w_qkv, w_out, segment_ids, end_positions, owners)
    return general_device(hidden, w_qkv, w_out, segment_ids, end_positions, owners)


def solution(mesh):
    placed = (
        P("groups", "gx"),
        P("gx", None),
        P("gx", None),
        P("groups"),
        P("groups"),
        P("groups"),
    )
    return jax.shard_map(
        per_device,
        mesh=mesh,
        in_specs=placed,
        out_specs=(P("groups", "gx"), P(("groups", "gx"), None)),
        check_vma=False,
    )
```
